128 devices in a mesh: span: 32 (over z, x, core), chan: 4 (over y).
Axes of the slice: x: 4, y: 4, z: 4, core: 2. Of those that a mesh axis runs over, the one named last changes fastest.
Arguments:
- noise: bfloat16 [3, 160, 2048, 512], P(None, 'chan', 'span'), may hold values from -6 to 6
- widths: int32 [512], replicated, may hold values from 0 to 3
- rms_profile: float32 [3, 512], replicated, may hold values from 0.3 to 1.5
- tile_owner: int32 [1024, 1], P('span'), may hold values from 0 to 31; in each aligned block of 32 rows (0 to 31, 32 to 63, ...) at most 2 rows name the same one
Outputs:
- inlet: float32 [32, 32, 2, 32, 3, 16, 64], P('span', None, None, 'chan')
The draws below stay inside these ranges and needn't reach their ends.
Inputs may be any that keep to these rules, and one draw needn't show every extreme that they name: `tile_owner`: among the 32 tiles of one vertical slab (an aligned block), no owner is named more than 2 times, and exactly 2 times in some block.
All inputs are finite; a program needn't handle non-finite values.
Results may differ from the reference program's by a relative error of at most 0.0027.
Values may be sent and summed in bfloat16 or wider, within the bound.
No kernel may reach another device: no remote copies, remote signals or barrier semaphores. Data moves between devices by JAX's collectives and lax.ppermute only.
A program may use at most 128 MiB of HBM per device.

```python
import math
import jax
import jax.numpy as jnp
import numpy as np
from jax import lax

Y = 2048
Z = 512
KT = 128
KY = 96
KZ = 48
NW = 4
TY = 64
NOUT = 32
NTIN = 160
ZD = 16
NTPD = 32
CAP = 2
NTILE = 1024
N_SPAN = 32


def set_ends(result, key, low, largest):
    place = [jax.random.randint(jax.random.fold_in(key, axis), (), 0, length) for axis, length in enumerate(result.shape)]
    longest = result.shape.index(max(result.shape))
    next_to = place[:longest] + [(place[longest] + 1) % result.shape[longest]] + place[longest + 1:]
    return result.at[tuple(place)].set(low).at[tuple(next_to)].set(largest)


def block_scale(stream_key, dims, cuts, low, top_value):
    factor_of = 1.0
    for dim, shards_of in cuts:
        draws = jax.random.uniform(jax.random.fold_in(jax.random.fold_in(stream_key, 6), dim), (shards_of,), jnp.float32, low / len(cuts), top_value / len(cuts))
        factor_of = factor_of * jnp.repeat(jnp.exp(draws), dims[dim] // shards_of).reshape((-1,) + (1,) * (len(dims) - 1 - dim))
    return factor_of


def assign_block(stream_key, own, number, rows, number_of, top, bound, lean):
    order = jax.random.permutation(stream_key, number_of)
    crowded, common = portions_of(number_of, rows * top, bound, lean, True), portions_of(number_of, rows * top, bound, lean, False)
    places = jnp.arange(number_of)

    def named(tallies, offset_by):
        used = int((tallies > 0).sum())
        fixed = max(1, used // 4)
        passed = fixed + (places - fixed + offset_by * (used - fixed)) % max(1, number_of - fixed)
        return jnp.zeros((number_of,), jnp.int32).at[order[jnp.where(places < fixed, places, passed)]].set(jnp.asarray(tallies, jnp.int32))

    tallies = jnp.where(number % 4 == 0, named(crowded, number // 4), named(common, number - number // 4 - 1))
    mixed = jax.random.permutation(jax.random.fold_in(own, 3), number_of)
    donor, taker = mixed[0:number_of // 2 * 2:2], mixed[1:number_of // 2 * 2:2]
    slack = jnp.minimum(tallies[donor] - 1, bound - tallies[taker]) // 2
    slack = jnp.where((donor == order[0]) | (taker == order[0]) | (tallies[taker] == 0), 0, jnp.maximum(slack, 0))
    passed = jax.random.randint(jax.random.fold_in(own, 4), (number_of // 2,), 0, 1 << 20) % (slack + 1)
    tallies = tallies.at[donor].add(-passed).at[taker].add(passed)
    items = jnp.searchsorted(jnp.cumsum(tallies), jnp.arange(rows * top), side="right").astype(jnp.int32)
    listing = items.reshape(top, rows).T
    listing = listing[jax.random.permutation(jax.random.fold_in(own, 1), rows)]
    offset_by = jax.random.randint(jax.random.fold_in(own, 2), (rows, 1), 0, top)
    return jnp.take_along_axis(listing, (jnp.arange(top)[None, :] + offset_by) % top, axis=1)


def portions_of(number_of, total, reach, slope, full):
    weights = [(1 << 20) // math.isqrt(standing ** slope) + 1 for standing in range(1, number_of + 1)]
    largest = reach if full else min(reach, max(-(-total // number_of), total * weights[0] // sum(weights)))
    least = 1 if total - largest >= number_of - 1 else 0
    holding, spare = [largest] + [least] * (number_of - 1), total - largest - least * (number_of - 1)
    while spare > 0:
        candidates = [i for i in range(1, number_of) if holding[i] < largest] or [i for i in range(1, number_of) if holding[i] < reach]
        whole, remaining = sum([weights[i] for i in candidates]), spare
        for i in candidates:
            addition = min(reach - holding[i], max(1, remaining * weights[i] // whole), spare)
            holding[i] = holding[i] + addition
            spare = spare - addition
    return np.array(holding)


def normal_values(key, shape, width, most, shards=(), kind=jnp.bfloat16):
    array = width * jax.random.normal(key, shape, jnp.float32)
    if shards:
        array = array * block_scale(key, shape, shards, -0.22, 0.18)
    return jnp.clip(array, -most, most).astype(kind)


def setup_inputs(seed: int = 0) -> dict:
    seeds = jax.random.split(jax.random.key(seed), 5)
    noise = normal_values(seeds[0], (3, NTIN, Y, Z), 1.0, 6.0, ((1, 4), (2, 32)))
    widths = set_ends(jax.random.randint(seeds[1], (Z,), 0, NW), jax.random.fold_in(seeds[1], 1), 0, NW - 1).astype(jnp.int32)
    rms_profile = jnp.clip(jnp.exp(jax.random.uniform(seeds[2], (3, Z), jnp.float32, math.log(0.3), math.log(1.5))), 0.3, 1.5)
    tile_owner_keys = jax.random.split(jax.random.fold_in(seeds[3], 1), NTILE // NTPD)
    tile_owner_turns = jax.random.permutation(jax.random.fold_in(seeds[3], 3), NTILE // NTPD)
    tile_owner = jax.vmap(lambda own, number: assign_block(jax.random.fold_in(seeds[3], 2), own, number, NTPD, N_SPAN, 1, CAP, 2))(tile_owner_keys, tile_owner_turns).reshape((NTILE, 1))
    return dict(noise=noise, widths=widths, rms_profile=rms_profile, tile_owner=tile_owner)


def gaussian(offset, length_scale):
    offset_f = jnp.asarray(offset).astype(jnp.float32)
    return jnp.exp(-math.pi * offset_f * offset_f / (2.0 * length_scale * length_scale))

def time_matrix():
    out_steps = jnp.arange(NOUT)[:, None]
    in_planes = jnp.arange(NTIN)[None, :]
    offset = in_planes - out_steps
    tap_norm = jnp.sqrt(jnp.sum(gaussian(jnp.arange(KT) - KT // 2, KT / 4.0) ** 2))
    inside = (offset >= 0) & (offset < KT)
    return jnp.where(inside, gaussian(offset - KT // 2, KT / 4.0) / tap_norm, 0.0).astype(jnp.bfloat16)

def vertical_filter_matrix(widths):
    out_cells = jnp.arange(Z)[:, None]
    in_cells = jnp.arange(Z)[None, :]
    offset = in_cells - out_cells
    length_scale = (KZ * (widths + 1)).astype(jnp.float32) / (4.0 * NW)
    tap_offsets = jnp.arange(KZ) - KZ // 2
    tap_norm = jnp.sqrt(lax.optimization_barrier(jnp.sum(gaussian(tap_offsets[None, :], length_scale[:, None]) ** 2, axis=1)))
    inside = (offset >= -(KZ // 2)) & (offset < KZ - KZ // 2)
    return jnp.where(inside, gaussian(offset, length_scale[:, None]) / tap_norm[:, None], 0.0)

def reference(noise, widths, rms_profile, tile_owner):
    time_taps = time_matrix()
    parts = []
    for component in range(3):
        flat = noise[component].reshape(NTIN, Y * Z)
        parts.append(jnp.dot(time_taps, flat, preferred_element_type=jnp.float32).reshape(NOUT, Y, Z))
    time_filtered_field = jnp.stack(parts, axis=1)
    vertical_weight_matrix = vertical_filter_matrix(widths)
    filtered_noise_field = jnp.einsum('eftg,qg->eftq', time_filtered_field, vertical_weight_matrix, precision=lax.Precision.HIGHEST)
    span_norm = jnp.sqrt(jnp.sum(gaussian(jnp.arange(KY) - KY // 2, KY / 4.0) ** 2))

    def add_tap(tap_index, running):
        weight = gaussian(tap_index - KY // 2, KY / 4.0) / span_norm
        return running + weight * jnp.roll(filtered_noise_field, KY // 2 - tap_index, axis=2)
    spanned = lax.fori_loop(0, KY, add_tap, jnp.zeros_like(filtered_noise_field))
    velocity = spanned * rms_profile[None, :, None, :]
    tiles = velocity.reshape(NOUT, 3, NTPD, TY, N_SPAN, ZD)
    tiles = jnp.transpose(tiles, (4, 2, 0, 1, 5, 3)).reshape(NTILE, NOUT, 3, ZD, TY)
    owner = tile_owner[:, 0]
    onehot = (owner[:, None] == jnp.arange(N_SPAN)[None, :]).astype(jnp.int32)
    blocked = onehot.reshape(N_SPAN, NTPD, N_SPAN)
    earlier = jnp.cumsum(blocked, axis=1) - blocked
    slot = lax.optimization_barrier(jnp.sum(earlier * blocked, axis=2)).reshape(NTILE)
    source = (jnp.arange(NTILE) // NTPD).astype(owner.dtype)
    inlet = jnp.zeros((N_SPAN, N_SPAN, CAP, NOUT, 3, ZD, TY), jnp.float32)
    return inlet.at[owner, source, slot].set(tiles)
```

```python
import functools
import math

import jax
import jax.numpy as jnp
import ml_dtypes
import numpy as np
from jax import lax
from jax.experimental import pallas as pl
from jax.experimental.pallas import tpu as pltpu
from jax.sharding import PartitionSpec as P

Y = 2048
Z = 512
KT = 128
KY = 96
KZ = 48
NW = 4
TY = 64
COMPS = 3
STEPS = 8
PLANES = 40
CHANS = 4
SPANS = 32
CAP = 2
ZD = Z // SPANS
ROWS = 16
GROUP = 4
LANES = GROUP * TY
VMEM_LIMIT = 56 * 1024 * 1024

PAIR_A = [(0, 1), (1, 0), (2, 3), (3, 2)]
PAIR_B = [(1, 2), (2, 1), (3, 0), (0, 3)]


def gaussian(offset, length_scale):
    return np.exp(-math.pi * offset * offset / (2.0 * length_scale * length_scale))


def time_taps():
    offset = np.arange(CHANS * PLANES)[None, :] - np.arange(CHANS * STEPS)[:, None]
    norm = np.sqrt(np.sum(gaussian(np.arange(KT) - KT // 2.0, KT / 4.0) ** 2))
    inside = (offset >= 0) & (offset < KT)
    return np.where(inside, gaussian(offset - KT // 2.0, KT / 4.0) / norm, 0.0)


def time_blocks():
    taps = time_taps().astype(np.float32).reshape(CHANS, STEPS, CHANS, PLANES)
    half = STEPS // 2
    blocks = []
    for d in range(CHANS):
        a, b, far = d ^ 1, CHANS - 1 - d, (d + 2) % CHANS
        first, second = slice(0, half), slice(half, STEPS)
        order = [(a, first), (far, first), (b, second), (far, second), (b, first), (a, second), (d, first), (d, second)]
        rows = np.concatenate([taps[block, steps, d] for block, steps in order])
        blocks.append(np.kron(rows, np.eye(ROWS, dtype=np.float32)))
    return np.stack(blocks).astype(ml_dtypes.bfloat16)


def split(values):
    high = values.astype(ml_dtypes.bfloat16)
    return high, (values - high.astype(np.float32)).astype(ml_dtypes.bfloat16)


def span_blocks():
    taps = gaussian(np.arange(KY) - KY // 2.0, KY / 4.0)
    taps = taps / np.sqrt(np.sum(taps**2))
    parts = []
    for shift in (-1, 0, 1):
        tap = np.arange(TY)[:, None] + TY * shift - np.arange(TY)[None, :] + KY // 2
        inside = (tap >= 0) & (tap < KY)
        band = np.where(inside, taps[np.clip(tap, 0, KY - 1)], 0.0).astype(np.float32)
        parts.append(np.kron(np.eye(GROUP, dtype=np.float32), band))
    return np.stack([np.stack(pair) for pair in zip(*[split(p) for p in parts])])


def vertical_filter_matrix(widths):
    def device_gaussian(offset, length_scale):
        offset_f = offset.astype(jnp.float32)
        return jnp.exp(-math.pi * offset_f * offset_f / (2.0 * length_scale * length_scale))

    offset = jnp.arange(Z)[None, :] - jnp.arange(Z)[:, None]
    length_scale = (KZ * (widths + 1)).astype(jnp.float32) / (4.0 * NW)
    tap_offsets = jnp.arange(KZ) - KZ // 2
    tap_norm = jnp.sqrt(
        jnp.sum(device_gaussian(tap_offsets[None, :], length_scale[:, None]) ** 2, axis=1)
    )
    inside = (offset >= -(KZ // 2)) & (offset < KZ - KZ // 2)
    return jnp.where(
        inside, device_gaussian(offset, length_scale[:, None]) / tap_norm[:, None], 0.0
    )


def time_kernel(chan_ref, taps_ref, noise_ref, to_a_ref, to_b_ref, kept_ref, own_ref):
    planes = noise_ref[...].reshape(PLANES * ROWS, Z)
    sums = jnp.dot(taps_ref[0], planes, preferred_element_type=jnp.float32)
    sums = sums.reshape(CHANS * STEPS, 1, ROWS, Z)
    to_a_ref[...] = sums[:8].astype(jnp.bfloat16)
    to_b_ref[...] = sums[8:16].astype(jnp.bfloat16)
    kept_ref[...] = sums[16:24]
    own_ref[...] = sums[24:]


def time_filter(noise, chan):
    part = pl.BlockSpec((STEPS, 1, ROWS, Z), lambda c, j, chan: (0, c, j, 0))
    shape = (STEPS, COMPS, TY, Z)
    return pl.pallas_call(
        time_kernel,
        grid_spec=pltpu.PrefetchScalarGridSpec(
            num_scalar_prefetch=1,
            grid=(COMPS, TY // ROWS),
            in_specs=[
                pl.BlockSpec((1, CHANS * STEPS * ROWS, PLANES * ROWS), lambda c, j, chan: (chan[0], 0, 0)),
                pl.BlockSpec((1, PLANES, ROWS, Z), lambda c, j, chan: (c, 0, j, 0)),
            ],
            out_specs=[part] * 4,
        ),
        out_shape=[
            jax.ShapeDtypeStruct(shape, jnp.bfloat16),
            jax.ShapeDtypeStruct(shape, jnp.bfloat16),
            jax.ShapeDtypeStruct(shape, jnp.float32),
            jax.ShapeDtypeStruct(shape, jnp.float32),
        ],
        compiler_params=pltpu.CompilerParams(vmem_limit_bytes=VMEM_LIMIT),
        name="time_filter",
    )(chan, time_blocks(), noise)


def vertical_kernel(high_ref, low_ref, own_ref, a_ref, b_ref, from_b_ref, from_a_ref, out_ref):
    half = STEPS // 2
    first = own_ref[:half] + a_ref[...].astype(jnp.float32) + from_b_ref[...].astype(jnp.float32)
    second = own_ref[half:] + b_ref[...].astype(jnp.float32) + from_a_ref[...].astype(jnp.float32)
    timed = jnp.concatenate([first, second]).reshape(STEPS * TY, Z)
    timed_high = timed.astype(jnp.bfloat16)
    timed_low = (timed - timed_high.astype(jnp.float32)).astype(jnp.bfloat16)

    def product(taps, values):
        return lax.dot_general(taps, values, (((1,), (1,)), ((), ())), preferred_element_type=jnp.float32)

    total = product(high_ref[...], timed_low) + product(low_ref[...], timed_high)
    total = total + product(high_ref[...], timed_high)
    out_ref[...] = total.astype(jnp.bfloat16)


def vertical_filter(taps_high, taps_low, own, from_a, from_b, second_b, second_a):
    half = pl.BlockSpec((STEPS // 2, 1, TY, Z), lambda c: (0, c, 0, 0))
    whole = pl.BlockSpec((Z, Z), lambda c: (0, 0))
    return pl.pallas_call(
        vertical_kernel,
        grid=(COMPS,),
        in_specs=[whole, whole, pl.BlockSpec((STEPS, 1, TY, Z), lambda c: (0, c, 0, 0)), half, half, half, half],
        out_specs=pl.BlockSpec((Z, STEPS * TY), lambda c: (0, c)),
        out_shape=jax.ShapeDtypeStruct((Z, COMPS * STEPS * TY), jnp.bfloat16),
        compiler_params=pltpu.CompilerParams(vmem_limit_bytes=VMEM_LIMIT),
        name="vertical_filter",
    )(taps_high, taps_low, own, from_a, from_b, second_b, second_a)


def span_kernel(owner_ref, taps_ref, rms_ref, x_ref, out_ref, count_ref, place_ref):
    def clear(o, carry):
        count_ref[o] = 0
        return carry

    lax.fori_loop(0, SPANS, clear, 0)

    def place(i, carry):
        owner = owner_ref[i]
        slot = count_ref[owner]
        count_ref[owner] = slot + 1
        place_ref[i] = owner * CAP + slot
        return carry

    lax.fori_loop(0, SPANS, place, 0)
    out_ref[...] = jnp.zeros_like(out_ref)
    for chunk in range(COMPS * STEPS // GROUP):
        lanes = pl.ds(chunk * LANES, LANES)
        x = x_ref[:, :, lanes]
        around = jnp.concatenate([x[SPANS - 1 :], x, x[:1]], axis=0).reshape((SPANS + 2) * ZD, LANES)
        total = None
        for part in (1, 0):
            for shift in range(3):
                rows = around[shift * ZD : (shift + SPANS) * ZD]
                term = jnp.dot(rows, taps_ref[part, shift], preferred_element_type=jnp.float32)
                total = term if total is None else total + term
        c = chunk * GROUP // STEPS
        velocity = total.reshape(SPANS, ZD, LANES) * rms_ref[:, c : c + 1][None]
        velocity = velocity.astype(jnp.bfloat16)
        for i in range(SPANS):
            out_ref[place_ref[i], :, lanes] = velocity[i]


def span_filter(owner, rms, moved):
    return pl.pallas_call(
        span_kernel,
        in_specs=[
            pl.BlockSpec(memory_space=pltpu.SMEM),
            pl.BlockSpec(memory_space=pltpu.VMEM),
            pl.BlockSpec(memory_space=pltpu.VMEM),
            pl.BlockSpec(memory_space=pltpu.VMEM),
        ],
        out_specs=pl.BlockSpec(memory_space=pltpu.VMEM),
        out_shape=jax.ShapeDtypeStruct((SPANS * CAP, ZD, COMPS * STEPS * TY), jnp.bfloat16),
        scratch_shapes=[pltpu.SMEM((SPANS,), jnp.int32), pltpu.SMEM((SPANS,), jnp.int32)],
        compiler_params=pltpu.CompilerParams(vmem_limit_bytes=VMEM_LIMIT),
        name="span_filter",
    )(owner, span_blocks(), rms, moved)


def inlet_kernel(x_ref, out_ref):
    for slot in range(CAP):
        for c in range(COMPS):
            for s in range(STEPS):
                first = (c * STEPS + s) * TY
                out_ref[0, :, slot, s, c] = x_ref[:, slot, :, first : first + TY].astype(jnp.float32)


def inlet_tiles(received):
    block = 4
    return pl.pallas_call(
        inlet_kernel,
        grid=(SPANS // block,),
        in_specs=[pl.BlockSpec((block, CAP, ZD, COMPS * STEPS * TY), lambda i: (i, 0, 0, 0))],
        out_specs=pl.BlockSpec((1, block, CAP, STEPS, COMPS, ZD, TY), lambda i: (0, i, 0, 0, 0, 0, 0)),
        out_shape=jax.ShapeDtypeStruct((1, SPANS, CAP, STEPS, COMPS, ZD, TY), jnp.float32),
        compiler_params=pltpu.CompilerParams(vmem_limit_bytes=VMEM_LIMIT),
        name="inlet_tiles",
    )(received)


def local(noise, widths, rms_profile, tile_owner):
    chan = lax.axis_index("chan").astype(jnp.int32).reshape(1)
    half = STEPS // 2
    to_a, to_b, kept, own = time_filter(noise, chan)
    from_a = lax.ppermute(to_a, "chan", PAIR_A)
    from_b = lax.ppermute(to_b, "chan", PAIR_B)
    for_b = (kept[:half] + from_a[half:].astype(jnp.float32)).astype(jnp.float16)
    for_a = (kept[half:] + from_b[half:].astype(jnp.float32)).astype(jnp.float16)
    second_b = lax.ppermute(for_b, "chan", PAIR_B).astype(jnp.float32)
    second_a = lax.ppermute(for_a, "chan", PAIR_A).astype(jnp.float32)
    taps = vertical_filter_matrix(widths)
    taps_high = lax.reduce_precision(taps, 8, 7)
    taps_low = (taps - taps_high).astype(jnp.bfloat16)
    taps_high = taps_high.astype(jnp.bfloat16)
    filtered = vertical_filter(taps_high, taps_low, own, from_a, from_b, second_b, second_a)
    filtered = filtered.reshape(SPANS, ZD, COMPS * STEPS * TY)
    moved = lax.all_to_all(filtered, "span", split_axis=0, concat_axis=0, tiled=True)
    rms = lax.dynamic_slice_in_dim(rms_profile, lax.axis_index("span") * ZD, ZD, 1).T
    sent = span_filter(tile_owner[:, 0], rms, moved)
    received = lax.all_to_all(sent, "span", split_axis=0, concat_axis=0, tiled=True)
    return inlet_tiles(received.reshape(SPANS, CAP, ZD, COMPS * STEPS * TY))


def solution(mesh):
    in_specs = (P(None, "chan", "span", None), P(), P(), P("span", None))
    out_specs = P("span", None, None, "chan", None, None, None)
    return jax.shard_map(local, mesh=mesh, in_specs=in_specs, out_specs=out_specs, check_vma=False)
```

```python
import functools
import math

import jax
import jax.numpy as jnp
import ml_dtypes
import numpy as np
from jax import lax
from jax.experimental import pallas as pl
from jax.experimental.pallas import tpu as pltpu
from jax.sharding import PartitionSpec as P

Y = 2048
Z = 512
KT = 128
KY = 96
KZ = 48
NW = 4
TY = 64
COMPS = 3
STEPS = 8
PLANES = 40
CHANS = 4
SPANS = 32
CAP = 2
ZD = Z // SPANS
ROWS = 16
BLOCK = 32
LANES = 2 * TY
WIDTH = STEPS * TY
MIB = 1024 * 1024
TIME_VMEM = 57 * MIB
VMEM = 16 * MIB

PAIR_A = [(0, 1), (1, 0), (2, 3), (3, 2)]
PAIR_B = [(1, 2), (2, 1), (3, 0), (0, 3)]


def gaussian(offset, length_scale):
    return np.exp(-math.pi * offset * offset / (2.0 * length_scale * length_scale))


def time_taps():
    offset = np.arange(CHANS * PLANES)[None, :] - np.arange(CHANS * STEPS)[:, None]
    norm = np.sqrt(np.sum(gaussian(np.arange(KT) - KT // 2.0, KT / 4.0) ** 2))
    inside = (offset >= 0) & (offset < KT)
    return np.where(inside, gaussian(offset - KT // 2.0, KT / 4.0) / norm, 0.0)


def time_blocks():
    taps = time_taps().astype(np.float32).reshape(CHANS, STEPS, CHANS, PLANES)
    half = STEPS // 2
    blocks = []
    for d in range(CHANS):
        a, b, far = d ^ 1, CHANS - 1 - d, (d + 2) % CHANS
        first, second = slice(0, half), slice(half, STEPS)
        order = [(a, first), (far, first), (b, second), (far, second), (b, first), (a, second), (d, first), (d, second)]
        rows = np.concatenate([taps[block, steps, d] for block, steps in order])
        blocks.append(np.kron(rows, np.eye(ROWS, dtype=np.float32)))
    return np.stack(blocks).astype(ml_dtypes.bfloat16)


def split(values):
    high = values.astype(ml_dtypes.bfloat16)
    return high, (values - high.astype(np.float32)).astype(ml_dtypes.bfloat16)


def span_blocks():
    taps = gaussian(np.arange(KY) - KY // 2.0, KY / 4.0)
    taps = taps / np.sqrt(np.sum(taps**2))
    blocks = np.zeros((4, 2, TY, 2, 2, TY), np.float32)
    for source in range(4):
        for target in range(2):
            shift = TY * (source - 1 - target)
            tap = np.arange(TY)[:, None] + shift - np.arange(TY)[None, :] + KY // 2
            band = np.where((tap >= 0) & (tap < KY), taps[np.clip(tap, 0, KY - 1)], 0.0)
            for step in range(2):
                blocks[source, step, :, target, step, :] = band
    return np.stack(split(blocks.reshape(2, 4 * TY, 4 * TY)))


def vertical_filter_matrix(widths):
    def device_gaussian(offset, length_scale):
        offset_f = offset.astype(jnp.float32)
        return jnp.exp(-math.pi * offset_f * offset_f / (2.0 * length_scale * length_scale))

    offset = jnp.arange(Z)[None, :] - jnp.arange(Z)[:, None]
    length_scale = (KZ * (widths + 1)).astype(jnp.float32) / (4.0 * NW)
    tap_offsets = jnp.arange(KZ) - KZ // 2
    tap_norm = jnp.sqrt(
        jnp.sum(device_gaussian(tap_offsets[None, :], length_scale[:, None]) ** 2, axis=1)
    )
    inside = (offset >= -(KZ // 2)) & (offset < KZ - KZ // 2)
    return jnp.where(
        inside, device_gaussian(offset, length_scale[:, None]) / tap_norm[:, None], 0.0
    )


def time_kernel(chan_ref, taps_ref, noise_ref, to_a_ref, to_b_ref, kept_ref, own_ref):
    for first in range(0, BLOCK, ROWS):
        rows = slice(first, first + ROWS)
        planes = noise_ref[:, :, rows].reshape(PLANES * ROWS, Z)
        sums = jnp.dot(taps_ref[0], planes, preferred_element_type=jnp.float32)
        sums = sums.reshape(CHANS * STEPS, 1, ROWS, Z)
        to_a_ref[:, :, rows] = sums[:8].astype(jnp.bfloat16)
        to_b_ref[:, :, rows] = sums[8:16].astype(jnp.bfloat16)
        kept_ref[:, :, rows] = sums[16:24]
        own_ref[:, :, rows] = sums[24:]


def time_filter(noise, chan, comp):
    part = pl.BlockSpec((STEPS, 1, BLOCK, Z), lambda j, chan: (0, 0, j, 0))
    shape = (STEPS, 1, TY, Z)
    return pl.pallas_call(
        time_kernel,
        grid_spec=pltpu.PrefetchScalarGridSpec(
            num_scalar_prefetch=1,
            grid=(TY // BLOCK,),
            in_specs=[
                pl.BlockSpec((1, CHANS * STEPS * ROWS, PLANES * ROWS), lambda j, chan: (chan[0], 0, 0)),
                pl.BlockSpec((1, PLANES, BLOCK, Z), lambda j, chan: (comp, 0, j, 0)),
            ],
            out_specs=[part] * 4,
        ),
        out_shape=[
            jax.ShapeDtypeStruct(shape, jnp.bfloat16),
            jax.ShapeDtypeStruct(shape, jnp.bfloat16),
            jax.ShapeDtypeStruct(shape, jnp.float32),
            jax.ShapeDtypeStruct(shape, jnp.float32),
        ],
        compiler_params=pltpu.CompilerParams(vmem_limit_bytes=TIME_VMEM),
        name="time_filter",
    )(chan, time_blocks(), noise)


def vertical_kernel(high_ref, low_ref, first_ref, second_ref, *refs):
    out_ref = refs[-1]
    timed = jnp.concatenate([first_ref[...], second_ref[...]]).reshape(STEPS * TY, Z)
    timed_high = timed.astype(jnp.bfloat16)
    timed_low = (timed - timed_high.astype(jnp.float32)).astype(jnp.bfloat16)

    def product(taps, values):
        return lax.dot_general(taps, values, (((1,), (1,)), ((), ())), preferred_element_type=jnp.float32)

    total = product(high_ref[...], timed_low) + product(low_ref[...], timed_high)
    total = total + product(high_ref[...], timed_high)
    out_ref[...] = total.astype(jnp.bfloat16).reshape(out_ref.shape)


def vertical_filter(taps, sums, shape, place, so_far=None):
    half = pl.BlockSpec((STEPS // 2, 1, TY, Z), lambda i: (0, 0, 0, 0))
    in_specs = [pl.BlockSpec((Z, Z), lambda i: (0, 0))] * 2 + [half] * 2
    if so_far is not None:
        in_specs.append(pl.BlockSpec(memory_space=pl.ANY))
    return pl.pallas_call(
        vertical_kernel,
        grid=(1,),
        in_specs=in_specs,
        out_specs=pl.BlockSpec((SPANS, ZD, WIDTH), lambda i: place),
        out_shape=jax.ShapeDtypeStruct(shape, jnp.bfloat16),
        input_output_aliases={} if so_far is None else {4: 0},
        compiler_params=pltpu.CompilerParams(vmem_limit_bytes=VMEM),
        name="vertical_filter",
    )(*taps, *sums, *([] if so_far is None else [so_far]))


def span_kernel(owner_ref, slot_ref, taps_ref, rms_ref, x_ref, *refs):
    out_ref = refs[-1]
    out_ref[...] = jnp.zeros_like(out_ref)
    pairs = SPANS // 2
    for first in range(0, WIDTH, LANES):
        lanes = slice(first, first + LANES)
        x = x_ref[:, :, lanes]
        around = jnp.concatenate([x[SPANS - 1 :], x, x[:1]], axis=0).reshape(pairs + 1, 2, ZD, LANES)
        total = None
        for part in (1, 0):
            for half in range(2):
                tiles = [around[half : half + pairs, tile] for tile in range(2)]
                rows = jnp.concatenate(tiles, axis=-1).reshape(pairs * ZD, 2 * LANES)
                term = jnp.dot(rows, taps_ref[part, half], preferred_element_type=jnp.float32)
                total = term if total is None else total + term
        velocity = (total.reshape(pairs, ZD, 2 * LANES) * rms_ref[...]).astype(jnp.bfloat16)
        for i in range(SPANS):
            target = (i % 2) * LANES
            rows = pl.ds(pl.multiple_of(slot_ref[i] * ZD, ZD), ZD)
            out_ref[owner_ref[i], rows, lanes] = velocity[i // 2, :, target : target + LANES]


def span_filter(owner, slot, rms, moved, place, first, comps, shape, so_far=None):
    row, column = place
    in_specs = [
        pl.BlockSpec(memory_space=pltpu.SMEM),
        pl.BlockSpec(memory_space=pltpu.SMEM),
        pl.BlockSpec((2, 2, 2 * LANES, 2 * LANES), lambda i: (0, 0, 0, 0)),
        pl.BlockSpec((1, ZD, 1), lambda i: (first + i, 0, 0)),
        pl.BlockSpec((SPANS, ZD, WIDTH), lambda i: (0, row, column + i)),
    ]
    if so_far is not None:
        in_specs.append(pl.BlockSpec(memory_space=pl.ANY))
    return pl.pallas_call(
        span_kernel,
        grid=(comps,),
        in_specs=in_specs,
        out_specs=pl.BlockSpec((SPANS, CAP * ZD, WIDTH), lambda i: (0, i, 0)),
        out_shape=jax.ShapeDtypeStruct(shape, jnp.bfloat16),
        input_output_aliases={} if so_far is None else {5: 0},
        compiler_params=pltpu.CompilerParams(vmem_limit_bytes=VMEM),
        name="span_filter",
    )(owner, slot, span_blocks(), rms, moved, *([] if so_far is None else [so_far]))


def inlet_kernel(x_ref, *refs):
    out_ref = refs[-1]
    for slot in range(CAP):
        for s in range(STEPS):
            tile = x_ref[:, slot * ZD : (slot + 1) * ZD, s * TY : (s + 1) * TY]
            out_ref[0, :, slot, s, 0] = tile.astype(jnp.float32)


def inlet_tiles(received, first, comps, so_far=None):
    block = 8
    in_specs = [pl.BlockSpec((block, CAP * ZD, WIDTH), lambda c, i: (i, c, 0))]
    if so_far is not None:
        in_specs.append(pl.BlockSpec(memory_space=pl.ANY))
    return pl.pallas_call(
        inlet_kernel,
        grid=(comps, SPANS // block),
        in_specs=in_specs,
        out_specs=pl.BlockSpec((1, block, CAP, STEPS, 1, ZD, TY), lambda c, i: (0, i, 0, 0, first + c, 0, 0)),
        out_shape=jax.ShapeDtypeStruct((1, SPANS, CAP, STEPS, COMPS, ZD, TY), jnp.float32),
        input_output_aliases={} if so_far is None else {1: 0},
        compiler_params=pltpu.CompilerParams(vmem_limit_bytes=VMEM),
        name="inlet_tiles",
    )(received, *([] if so_far is None else [so_far]))


def after(values, others):
    return lax.optimization_barrier((*values, *others))[: len(values)]


def first_exchange(to_a, to_b):
    return lax.ppermute(to_a, "chan", PAIR_A), lax.ppermute(to_b, "chan", PAIR_B)


def for_second_exchange(kept, from_a, from_b):
    half = STEPS // 2
    for_b = (kept[:half] + from_a[half:].astype(jnp.float32)).astype(jnp.float16)
    for_a = (kept[half:] + from_b[half:].astype(jnp.float32)).astype(jnp.float16)
    return for_b, for_a


def second_exchange(for_b, for_a):
    return lax.ppermute(for_b, "chan", PAIR_B), lax.ppermute(for_a, "chan", PAIR_A)


def summed(own, from_a, from_b, second_b, second_a):
    half = STEPS // 2
    first = own[:half] + from_a[:half].astype(jnp.float32) + second_b.astype(jnp.float32)
    second = own[half:] + from_b[:half].astype(jnp.float32) + second_a.astype(jnp.float32)
    return first, second


def along_span(values):
    return lax.all_to_all(values, "span", split_axis=0, concat_axis=0, tiled=True)


def local(noise, widths, rms_profile, tile_owner):
    chan = lax.axis_index("chan").astype(jnp.int32).reshape(1)
    taps = vertical_filter_matrix(widths)
    taps_high = lax.reduce_precision(taps, 8, 7)
    taps_low = (taps - taps_high).astype(jnp.bfloat16)
    taps = (taps_high.astype(jnp.bfloat16), taps_low)
    rms = lax.dynamic_slice_in_dim(rms_profile, lax.axis_index("span") * ZD, ZD, 1)[:, :, None]
    owner = tile_owner[:, 0]
    tile = jnp.arange(SPANS, dtype=jnp.int32)
    earlier = (owner[:, None] == owner[None, :]) & (tile[None, :] < tile[:, None])
    slot = jnp.sum(earlier.astype(jnp.int32), axis=1)

    partial = [time_filter(noise, chan, c) for c in range(COMPS)]
    early = (*partial[1], *partial[2], *taps, owner, slot, rms)
    sums, got = [], None
    for to_a, to_b, kept, own in partial:
        if got is None:
            got = after(first_exchange(to_a, to_b), early)
        else:
            got = first_exchange(*after((to_a, to_b), got))
        sums.append(summed(own, *got, *second_exchange(*for_second_exchange(kept, *got))))

    planes = None
    for c in range(2):
        planes = vertical_filter(taps, sums[c], (SPANS, ZD, 2 * WIDTH), (0, 0, c), planes)
    moved = along_span(planes)
    shape = (SPANS, 2 * CAP * ZD + ZD, WIDTH)
    mixed = vertical_filter(taps, sums[2], shape, (0, 2 * CAP, 0))
    mixed = along_span(span_filter(owner, slot, rms, moved, (0, 0), 0, 2, shape, mixed))
    last = span_filter(owner, slot, rms, mixed, (2 * CAP, 0), 2, 1, (SPANS, CAP * ZD, WIDTH))
    last = along_span(last)
    return inlet_tiles(last, 2, 1, inlet_tiles(mixed, 0, 2))


def solution(mesh):
    in_specs = (P(None, "chan", "span", None), P(), P(), P("span", None))
    out_specs = P("span", None, None, "chan", None, None, None)
    return jax.shard_map(local, mesh=mesh, in_specs=in_specs, out_specs=out_specs, check_vma=False)
```

```python
import functools
import math

import jax
import jax.numpy as jnp
import ml_dtypes
import numpy as np
from jax import lax
from jax.experimental import pallas as pl
from jax.experimental.pallas import tpu as pltpu
from jax.sharding import PartitionSpec as P

Y = 2048
Z = 512
KT = 128
KY = 96
KZ = 48
NW = 4
TY = 64
COMPS = 3
STEPS = 8
PLANES = 40
CHANS = 4
SPANS = 32
CAP = 2
ZD = Z // SPANS
ROWS = 16
BLOCK = 32
LANES = 2 * TY
WIDTH = STEPS * TY
MIB = 1024 * 1024
TIME_VMEM = 57 * MIB
VMEM = 16 * MIB

PAIR_A = [(0, 1), (1, 0), (2, 3), (3, 2)]
PAIR_B = [(1, 2), (2, 1), (3, 0), (0, 3)]


def gaussian(offset, length_scale):
    return np.exp(-math.pi * offset * offset / (2.0 * length_scale * length_scale))


def time_taps():
    offset = np.arange(CHANS * PLANES)[None, :] - np.arange(CHANS * STEPS)[:, None]
    norm = np.sqrt(np.sum(gaussian(np.arange(KT) - KT // 2.0, KT / 4.0) ** 2))
    inside = (offset >= 0) & (offset < KT)
    return np.where(inside, gaussian(offset - KT // 2.0, KT / 4.0) / norm, 0.0)


def time_blocks():
    taps = time_taps().astype(np.float32).reshape(CHANS, STEPS, CHANS, PLANES)
    half = STEPS // 2
    blocks = []
    for d in range(CHANS):
        a, b, far = d ^ 1, CHANS - 1 - d, (d + 2) % CHANS
        first, second = slice(0, half), slice(half, STEPS)
        order = [(a, first), (far, first), (b, second), (far, second), (b, first), (a, second), (d, first), (d, second)]
        rows = np.concatenate([taps[block, steps, d] for block, steps in order])
        blocks.append(np.kron(rows, np.eye(ROWS, dtype=np.float32)))
    return np.stack(blocks).astype(ml_dtypes.bfloat16)


def split(values):
    high = values.astype(ml_dtypes.bfloat16)
    return high, (values - high.astype(np.float32)).astype(ml_dtypes.bfloat16)


def span_bands():
    taps = gaussian(np.arange(KY) - KY // 2.0, KY / 4.0)
    taps = taps / np.sqrt(np.sum(taps**2))
    bands = np.zeros((3, 2, TY, 2, TY), np.float32)
    for shift in range(3):
        tap = np.arange(TY)[:, None] + TY * (shift - 1) - np.arange(TY)[None, :] + KY // 2
        for step in range(2):
            bands[shift, step, :, step, :] = np.where((tap >= 0) & (tap < KY), taps[np.clip(tap, 0, KY - 1)], 0.0)
    return np.stack(split(bands.reshape(3, 2, TY, LANES)))


def vertical_filter_matrix(widths):
    def device_gaussian(offset, length_scale):
        offset_f = offset.astype(jnp.float32)
        return jnp.exp(-math.pi * offset_f * offset_f / (2.0 * length_scale * length_scale))

    offset = jnp.arange(Z)[None, :] - jnp.arange(Z)[:, None]
    length_scale = (KZ * (widths + 1)).astype(jnp.float32) / (4.0 * NW)
    tap_offsets = jnp.arange(KZ) - KZ // 2
    tap_norm = jnp.sqrt(
        jnp.sum(device_gaussian(tap_offsets[None, :], length_scale[:, None]) ** 2, axis=1)
    )
    inside = (offset >= -(KZ // 2)) & (offset < KZ - KZ // 2)
    return jnp.where(
        inside, device_gaussian(offset, length_scale[:, None]) / tap_norm[:, None], 0.0
    )


def time_kernel(chan_ref, taps_ref, noise_ref, *out_refs):
    for first in range(0, BLOCK, ROWS):
        rows = slice(first, first + ROWS)
        planes = noise_ref[:, :, rows].reshape(PLANES * ROWS, Z)
        sums = jnp.dot(taps_ref[0], planes, preferred_element_type=jnp.float32)
        sums = sums.reshape(2, STEPS, 1, ROWS, Z)
        for block, out_ref in enumerate(out_refs):
            out_ref[:, :, rows] = sums[block].astype(out_ref.dtype)


def time_filter(noise, chan, comp, leaving):
    out = pl.BlockSpec((STEPS, 1, BLOCK, Z), lambda j, chan: (0, 0, j, 0))
    part = 0 if leaving else 1
    kind = jnp.bfloat16 if leaving else jnp.float32
    return pl.pallas_call(
        time_kernel,
        grid_spec=pltpu.PrefetchScalarGridSpec(
            num_scalar_prefetch=1,
            grid=(TY // BLOCK,),
            in_specs=[
                pl.BlockSpec((1, 2 * STEPS * ROWS, PLANES * ROWS), lambda j, chan: (chan[0], part, 0)),
                pl.BlockSpec((1, PLANES, BLOCK, Z), lambda j, chan: (comp, 0, j, 0)),
            ],
            out_specs=[out] * 2,
        ),
        out_shape=[jax.ShapeDtypeStruct((STEPS, 1, TY, Z), kind)] * 2,
        compiler_params=pltpu.CompilerParams(vmem_limit_bytes=TIME_VMEM),
        name="time_filter",
    )(chan, time_blocks(), noise)


def vertical_kernel(high_ref, low_ref, first_ref, second_ref, *refs):
    out_ref = refs[-1]
    timed = jnp.concatenate([first_ref[...], second_ref[...]]).reshape(STEPS * TY, Z)
    timed_high = timed.astype(jnp.bfloat16)
    timed_low = (timed - timed_high.astype(jnp.float32)).astype(jnp.bfloat16)

    def product(taps, values):
        return lax.dot_general(taps, values, (((1,), (1,)), ((), ())), preferred_element_type=jnp.float32)

    total = product(high_ref[...], timed_low) + product(low_ref[...], timed_high)
    total = total + product(high_ref[...], timed_high)
    out_ref[...] = total.astype(jnp.bfloat16).reshape(out_ref.shape)


def vertical_filter(taps, sums, shape, place, so_far=None):
    half = pl.BlockSpec((STEPS // 2, 1, TY, Z), lambda i: (0, 0, 0, 0))
    in_specs = [pl.BlockSpec((Z, Z), lambda i: (0, 0))] * 2 + [half] * 2
    if so_far is not None:
        in_specs.append(pl.BlockSpec(memory_space=pl.ANY))
    return pl.pallas_call(
        vertical_kernel,
        grid=(1,),
        in_specs=in_specs,
        out_specs=pl.BlockSpec((SPANS, ZD, WIDTH), lambda i: place),
        out_shape=jax.ShapeDtypeStruct(shape, jnp.bfloat16),
        input_output_aliases={} if so_far is None else {4: 0},
        compiler_params=pltpu.CompilerParams(vmem_limit_bytes=VMEM),
        name="vertical_filter",
    )(*taps, *sums, *([] if so_far is None else [so_far]))


def span_kernel(keep, owner_ref, slot_ref, bands_ref, rms_ref, x_ref, *refs):
    if keep:
        whole_ref, out_ref, kept_ref, taps_ref, sem = refs
        copy = pltpu.make_async_copy(whole_ref.at[:, : kept_ref.shape[1]], kept_ref, sem)
        copy.start()
    else:
        out_ref, taps_ref, sem = refs[-3:]

    @pl.when(pl.program_id(0) == 0)
    def _():
        for part in range(2):
            for source in range(4):
                for step in range(2):
                    rows = pl.ds((source % 2) * LANES + step * TY, TY)
                    for target in range(2):
                        shift = source - target
                        columns = pl.ds(target * LANES, LANES)
                        band = bands_ref[part, shift, step] if 0 <= shift < 3 else jnp.zeros((TY, LANES), jnp.bfloat16)
                        taps_ref[part, source // 2, rows, columns] = band

    out_ref[...] = jnp.zeros_like(out_ref)
    pairs = SPANS // 2
    for first in range(0, WIDTH, LANES):
        lanes = slice(first, first + LANES)
        x = x_ref[:, :, lanes]
        around = jnp.concatenate([x[SPANS - 1 :], x, x[:1]], axis=0).reshape(pairs + 1, 2, ZD, LANES)
        total = None
        for part in (1, 0):
            for half in range(2):
                tiles = [around[half : half + pairs, tile] for tile in range(2)]
                rows = jnp.concatenate(tiles, axis=-1).reshape(pairs * ZD, 2 * LANES)
                term = jnp.dot(rows, taps_ref[part, half], preferred_element_type=jnp.float32)
                total = term if total is None else total + term
        velocity = (total.reshape(pairs, ZD, 2 * LANES) * rms_ref[...]).astype(jnp.bfloat16)
        for i in range(SPANS):
            target = (i % 2) * LANES
            rows = pl.ds(pl.multiple_of(slot_ref[i] * ZD, ZD), ZD)
            out_ref[owner_ref[i], rows, lanes] = velocity[i // 2, :, target : target + LANES]
    if keep:
        copy.wait()


def span_filter(owner, slot, rms, moved, place, first, comps, shape, so_far=None, keep=0):
    row, column = place
    in_specs = [
        pl.BlockSpec(memory_space=pltpu.SMEM),
        pl.BlockSpec(memory_space=pltpu.SMEM),
        pl.BlockSpec((2, 3, 2, TY, LANES), lambda i: (0, 0, 0, 0, 0)),
        pl.BlockSpec((1, ZD, 1), lambda i: (first + i, 0, 0)),
        pl.BlockSpec((SPANS, ZD, WIDTH), lambda i: (0, row, column + i)),
    ]
    out_specs = [pl.BlockSpec((SPANS, CAP * ZD, WIDTH), lambda i: (0, i, 0))]
    out_shape = [jax.ShapeDtypeStruct(shape, jnp.bfloat16)]
    more = []
    if so_far is not None:
        in_specs.append(pl.BlockSpec(memory_space=pl.ANY))
        more.append(so_far)
    if keep:
        in_specs.append(pl.BlockSpec(memory_space=pl.ANY))
        more.append(moved)
        out_specs.append(pl.BlockSpec(memory_space=pl.ANY))
        out_shape.append(jax.ShapeDtypeStruct((SPANS, keep, WIDTH), jnp.bfloat16))
    return pl.pallas_call(
        functools.partial(span_kernel, keep > 0),
        grid=(comps,),
        in_specs=in_specs,
        out_specs=out_specs,
        out_shape=out_shape,
        input_output_aliases={} if so_far is None else {5: 0},
        scratch_shapes=[pltpu.VMEM((2, 2, 2 * LANES, 2 * LANES), jnp.bfloat16), pltpu.SemaphoreType.DMA],
        compiler_params=pltpu.CompilerParams(vmem_limit_bytes=VMEM),
        name="span_filter",
    )(owner, slot, span_bands(), rms, moved, *more)


def inlet_kernel(x_ref, *refs):
    out_ref = refs[-1]
    for slot in range(CAP):
        for s in range(STEPS):
            tile = x_ref[:, slot * ZD : (slot + 1) * ZD, s * TY : (s + 1) * TY]
            out_ref[0, :, slot, s, 0] = tile.astype(jnp.float32)


def inlet_tiles(received, first, comps, so_far=None):
    block = 8
    in_specs = [pl.BlockSpec((block, CAP * ZD, WIDTH), lambda c, i: (i, c, 0))]
    if so_far is not None:
        in_specs.append(pl.BlockSpec(memory_space=pl.ANY))
    return pl.pallas_call(
        inlet_kernel,
        grid=(comps, SPANS // block),
        in_specs=in_specs,
        out_specs=pl.BlockSpec((1, block, CAP, STEPS, 1, ZD, TY), lambda c, i: (0, i, 0, 0, first + c, 0, 0)),
        out_shape=jax.ShapeDtypeStruct((1, SPANS, CAP, STEPS, COMPS, ZD, TY), jnp.float32),
        input_output_aliases={} if so_far is None else {1: 0},
        compiler_params=pltpu.CompilerParams(vmem_limit_bytes=VMEM),
        name="inlet_tiles",
    )(received, *([] if so_far is None else [so_far]))


def after(values, others):
    return lax.optimization_barrier((*values, *others))[: len(values)] if others else values


def first_exchange(to_a, to_b):
    return lax.ppermute(to_a, "chan", PAIR_A), lax.ppermute(to_b, "chan", PAIR_B)


def for_second_exchange(kept, from_a, from_b):
    half = STEPS // 2
    for_b = (kept[:half] + from_a[half:].astype(jnp.float32)).astype(jnp.float16)
    for_a = (kept[half:] + from_b[half:].astype(jnp.float32)).astype(jnp.float16)
    return for_b, for_a


def second_exchange(for_b, for_a):
    return lax.ppermute(for_b, "chan", PAIR_B), lax.ppermute(for_a, "chan", PAIR_A)


def summed(own, from_a, from_b, second_b, second_a):
    half = STEPS // 2
    first = own[:half] + from_a[:half].astype(jnp.float32) + second_b.astype(jnp.float32)
    second = own[half:] + from_b[:half].astype(jnp.float32) + second_a.astype(jnp.float32)
    return first, second


def along_span(values):
    return lax.all_to_all(values, "span", split_axis=0, concat_axis=0, tiled=True)


def local(noise, widths, rms_profile, tile_owner):
    chan = lax.axis_index("chan").astype(jnp.int32).reshape(1)
    taps = vertical_filter_matrix(widths)
    taps_high = lax.reduce_precision(taps, 8, 7)
    taps_low = (taps - taps_high).astype(jnp.bfloat16)
    taps = (taps_high.astype(jnp.bfloat16), taps_low)
    rms = lax.dynamic_slice_in_dim(rms_profile, lax.axis_index("span") * ZD, ZD, 1)[:, :, None]
    owner = tile_owner[:, 0]
    tile = jnp.arange(SPANS, dtype=jnp.int32)
    earlier = (owner[:, None] == owner[None, :]) & (tile[None, :] < tile[:, None])
    slot = jnp.sum(earlier.astype(jnp.int32), axis=1)

    leave0, leave1 = [time_filter(noise, chan, c, True) for c in range(2)]
    stay0 = time_filter(noise, chan, 0, False)
    got0 = after(first_exchange(*leave0), (*leave1, *stay0, *taps, owner, slot, rms))
    got1 = first_exchange(*after(leave1, got0))
    sends0 = for_second_exchange(stay0[0], *got0)
    (chan,) = after((chan,), sends0)
    stay1, stay2 = [time_filter(noise, chan, c, False) for c in (1, 2)]
    leave2 = time_filter(noise, chan, 2, True)
    got1 = after(got1, (*stay1, *stay2, *leave2))
    sends1 = for_second_exchange(stay1[0], *got1)
    got2 = first_exchange(*after(leave2, sends1))
    sends2 = for_second_exchange(stay2[0], *got2)
    sums = [
        summed(stay[1], *got, *second_exchange(*sends))
        for stay, got, sends in ((stay0, got0, sends0), (stay1, got1, sends1), (stay2, got2, sends2))
    ]

    planes = None
    for c in range(2):
        planes = vertical_filter(taps, sums[c], (SPANS, ZD, 2 * WIDTH), (0, 0, c), planes)
    moved = along_span(planes)
    shape = (SPANS, 2 * CAP * ZD + ZD, WIDTH)
    mixed = vertical_filter(taps, sums[2], shape, (0, 2 * CAP, 0))
    mixed = along_span(span_filter(owner, slot, rms, moved, (0, 0), 0, 2, shape, mixed)[0])
    last, tiles = span_filter(
        owner, slot, rms, mixed, (2 * CAP, 0), 2, 1, (SPANS, CAP * ZD, WIDTH), keep=2 * CAP * ZD
    )
    return inlet_tiles(along_span(last), 2, 1, inlet_tiles(tiles, 0, 2))


def solution(mesh):
    in_specs = (P(None, "chan", "span", None), P(), P(), P("span", None))
    out_specs = P("span", None, None, "chan", None, None, None)
    return jax.shard_map(local, mesh=mesh, in_specs=in_specs, out_specs=out_specs, check_vma=False)
```

```python
import functools
import math

import jax
import jax.numpy as jnp
import ml_dtypes
import numpy as np
from jax import lax
from jax.experimental import pallas as pl
from jax.experimental.pallas import tpu as pltpu
from jax.sharding import PartitionSpec as P

Y = 2048
Z = 512
KT = 128
KY = 96
KZ = 48
NW = 4
TY = 64
COMPS = 3
STEPS = 8
PLANES = 40
CHANS = 4
SPANS = 32
CAP = 2
ZD = Z // SPANS
ROWS = 16
BLOCK = 32
LANES = 2 * TY
WIDTH = STEPS * TY
MIB = 1024 * 1024
TIME_VMEM = 57 * MIB
VMEM = 16 * MIB

PAIR_A = [(0, 1), (1, 0), (2, 3), (3, 2)]
PAIR_B = [(1, 2), (2, 1), (3, 0), (0, 3)]


def gaussian(offset, length_scale):
    return np.exp(-math.pi * offset * offset / (2.0 * length_scale * length_scale))


def time_taps():
    offset = np.arange(CHANS * PLANES)[None, :] - np.arange(CHANS * STEPS)[:, None]
    norm = np.sqrt(np.sum(gaussian(np.arange(KT) - KT // 2.0, KT / 4.0) ** 2))
    inside = (offset >= 0) & (offset < KT)
    return np.where(inside, gaussian(offset - KT // 2.0, KT / 4.0) / norm, 0.0)


def time_blocks():
    taps = time_taps().astype(np.float32).reshape(CHANS, STEPS, CHANS, PLANES)
    half = STEPS // 2
    blocks = []
    for d in range(CHANS):
        a, b, far = d ^ 1, CHANS - 1 - d, (d + 2) % CHANS
        first, second = slice(0, half), slice(half, STEPS)
        order = [(a, first), (far, first), (b, second), (far, second), (b, first), (a, second), (d, first), (d, second)]
        rows = np.concatenate([taps[block, steps, d] for block, steps in order])
        blocks.append(np.kron(rows, np.eye(ROWS, dtype=np.float32)))
    return np.stack(blocks).astype(ml_dtypes.bfloat16)


def split(values):
    high = values.astype(ml_dtypes.bfloat16)
    return high, (values - high.astype(np.float32)).astype(ml_dtypes.bfloat16)


def span_bands():
    taps = gaussian(np.arange(KY) - KY // 2.0, KY / 4.0)
    taps = taps / np.sqrt(np.sum(taps**2))
    bands = np.zeros((3, 2, TY, 2, TY), np.float32)
    for shift in range(3):
        tap = np.arange(TY)[:, None] + TY * (shift - 1) - np.arange(TY)[None, :] + KY // 2
        for step in range(2):
            bands[shift, step, :, step, :] = np.where((tap >= 0) & (tap < KY), taps[np.clip(tap, 0, KY - 1)], 0.0)
    return np.stack(split(bands.reshape(3, 2, TY, LANES)))


def vertical_filter_matrix(widths):
    def device_gaussian(offset, length_scale):
        offset_f = offset.astype(jnp.float32)
        return jnp.exp(-math.pi * offset_f * offset_f / (2.0 * length_scale * length_scale))

    offset = jnp.arange(Z)[None, :] - jnp.arange(Z)[:, None]
    length_scale = (KZ * (widths + 1)).astype(jnp.float32) / (4.0 * NW)
    tap_offsets = jnp.arange(KZ) - KZ // 2
    tap_norm = jnp.sqrt(
        jnp.sum(device_gaussian(tap_offsets[None, :], length_scale[:, None]) ** 2, axis=1)
    )
    inside = (offset >= -(KZ // 2)) & (offset < KZ - KZ // 2)
    return jnp.where(
        inside, device_gaussian(offset, length_scale[:, None]) / tap_norm[:, None], 0.0
    )


def time_kernel(chan_ref, taps_ref, noise_ref, *out_refs):
    for first in range(0, BLOCK, ROWS):
        rows = slice(first, first + ROWS)
        planes = noise_ref[:, :, rows].reshape(PLANES * ROWS, Z)
        sums = jnp.dot(taps_ref[0], planes, preferred_element_type=jnp.float32)
        sums = sums.reshape(2, STEPS, 1, ROWS, Z)
        for block, out_ref in enumerate(out_refs):
            out_ref[:, :, rows] = sums[block].astype(out_ref.dtype)


def time_filter(noise, chan, comp, leaving):
    out = pl.BlockSpec((STEPS, 1, BLOCK, Z), lambda j, chan: (0, 0, j, 0))
    part = 0 if leaving else 1
    kind = jnp.bfloat16 if leaving and comp == 0 else jnp.float32
    return pl.pallas_call(
        time_kernel,
        grid_spec=pltpu.PrefetchScalarGridSpec(
            num_scalar_prefetch=1,
            grid=(TY // BLOCK,),
            in_specs=[
                pl.BlockSpec((1, 2 * STEPS * ROWS, PLANES * ROWS), lambda j, chan: (chan[0], part, 0)),
                pl.BlockSpec((1, PLANES, BLOCK, Z), lambda j, chan: (comp, 0, j, 0)),
            ],
            out_specs=[out] * 2,
        ),
        out_shape=[jax.ShapeDtypeStruct((STEPS, 1, TY, Z), kind)] * 2,
        compiler_params=pltpu.CompilerParams(vmem_limit_bytes=TIME_VMEM),
        name="time_filter",
    )(chan, time_blocks(), noise)


def vertical_kernel(high_ref, low_ref, first_ref, second_ref, *refs):
    out_ref = refs[-1]
    timed = jnp.concatenate([first_ref[...], second_ref[...]]).reshape(STEPS * TY, Z)
    timed_high = timed.astype(jnp.bfloat16)
    timed_low = (timed - timed_high.astype(jnp.float32)).astype(jnp.bfloat16)

    def product(taps, values):
        return lax.dot_general(taps, values, (((1,), (1,)), ((), ())), preferred_element_type=jnp.float32)

    total = product(high_ref[...], timed_low) + product(low_ref[...], timed_high)
    total = total + product(high_ref[...], timed_high)
    out_ref[...] = total.astype(jnp.bfloat16).reshape(out_ref.shape)


def vertical_filter(taps, sums, shape, place, so_far=None):
    half = pl.BlockSpec((STEPS // 2, 1, TY, Z), lambda i: (0, 0, 0, 0))
    in_specs = [pl.BlockSpec((Z, Z), lambda i: (0, 0))] * 2 + [half] * 2
    if so_far is not None:
        in_specs.append(pl.BlockSpec(memory_space=pl.ANY))
    return pl.pallas_call(
        vertical_kernel,
        grid=(1,),
        in_specs=in_specs,
        out_specs=pl.BlockSpec((SPANS, ZD, WIDTH), lambda i: place),
        out_shape=jax.ShapeDtypeStruct(shape, jnp.bfloat16),
        input_output_aliases={} if so_far is None else {4: 0},
        compiler_params=pltpu.CompilerParams(vmem_limit_bytes=VMEM),
        name="vertical_filter",
    )(*taps, *sums, *([] if so_far is None else [so_far]))


def span_kernel(keep, owner_ref, slot_ref, bands_ref, rms_ref, x_ref, *refs):
    if keep:
        whole_ref, out_ref, kept_ref, taps_ref, sem = refs
        copy = pltpu.make_async_copy(whole_ref.at[:, : kept_ref.shape[1]], kept_ref, sem)
        copy.start()
    else:
        out_ref, taps_ref, sem = refs[-3:]

    @pl.when(pl.program_id(0) == 0)
    def _():
        for part in range(2):
            for source in range(4):
                for step in range(2):
                    rows = pl.ds((source % 2) * LANES + step * TY, TY)
                    for target in range(2):
                        shift = source - target
                        columns = pl.ds(target * LANES, LANES)
                        band = bands_ref[part, shift, step] if 0 <= shift < 3 else jnp.zeros((TY, LANES), jnp.bfloat16)
                        taps_ref[part, source // 2, rows, columns] = band

    out_ref[...] = jnp.zeros_like(out_ref)
    pairs = SPANS // 2
    for first in range(0, WIDTH, LANES):
        lanes = slice(first, first + LANES)
        x = x_ref[:, :, lanes]
        around = jnp.concatenate([x[SPANS - 1 :], x, x[:1]], axis=0).reshape(pairs + 1, 2, ZD, LANES)
        total = None
        for part in (1, 0):
            for half in range(2):
                tiles = [around[half : half + pairs, tile] for tile in range(2)]
                rows = jnp.concatenate(tiles, axis=-1).reshape(pairs * ZD, 2 * LANES)
                term = jnp.dot(rows, taps_ref[part, half], preferred_element_type=jnp.float32)
                total = term if total is None else total + term
        velocity = (total.reshape(pairs, ZD, 2 * LANES) * rms_ref[...]).astype(jnp.bfloat16)
        for i in range(SPANS):
            target = (i % 2) * LANES
            rows = pl.ds(pl.multiple_of(slot_ref[i] * ZD, ZD), ZD)
            out_ref[owner_ref[i], rows, lanes] = velocity[i // 2, :, target : target + LANES]
    if keep:
        copy.wait()


def span_filter(owner, slot, rms, moved, place, first, comps, shape, so_far=None, keep=0):
    row, column = place
    in_specs = [
        pl.BlockSpec(memory_space=pltpu.SMEM),
        pl.BlockSpec(memory_space=pltpu.SMEM),
        pl.BlockSpec((2, 3, 2, TY, LANES), lambda i: (0, 0, 0, 0, 0)),
        pl.BlockSpec((1, ZD, 1), lambda i: (first + i, 0, 0)),
        pl.BlockSpec((SPANS, ZD, WIDTH), lambda i: (0, row, column + i)),
    ]
    out_specs = [pl.BlockSpec((SPANS, CAP * ZD, WIDTH), lambda i: (0, i, 0))]
    out_shape = [jax.ShapeDtypeStruct(shape, jnp.bfloat16)]
    more = []
    if so_far is not None:
        in_specs.append(pl.BlockSpec(memory_space=pl.ANY))
        more.append(so_far)
    if keep:
        in_specs.append(pl.BlockSpec(memory_space=pl.ANY))
        more.append(moved)
        out_specs.append(pl.BlockSpec(memory_space=pl.ANY))
        out_shape.append(jax.ShapeDtypeStruct((SPANS, keep, WIDTH), jnp.bfloat16))
    return pl.pallas_call(
        functools.partial(span_kernel, keep > 0),
        grid=(comps,),
        in_specs=in_specs,
        out_specs=out_specs,
        out_shape=out_shape,
        input_output_aliases={} if so_far is None else {5: 0},
        scratch_shapes=[pltpu.VMEM((2, 2, 2 * LANES, 2 * LANES), jnp.bfloat16), pltpu.SemaphoreType.DMA],
        compiler_params=pltpu.CompilerParams(vmem_limit_bytes=VMEM),
        name="span_filter",
    )(owner, slot, span_bands(), rms, moved, *more)


def inlet_kernel(x_ref, *refs):
    out_ref = refs[-1]
    for slot in range(CAP):
        for s in range(STEPS):
            tile = x_ref[:, slot * ZD : (slot + 1) * ZD, s * TY : (s + 1) * TY]
            out_ref[0, :, slot, s, 0] = tile.astype(jnp.float32)


def inlet_tiles(received, first, comps, so_far=None):
    block = 8
    in_specs = [pl.BlockSpec((block, CAP * ZD, WIDTH), lambda c, i: (i, c, 0))]
    if so_far is not None:
        in_specs.append(pl.BlockSpec(memory_space=pl.ANY))
    return pl.pallas_call(
        inlet_kernel,
        grid=(comps, SPANS // block),
        in_specs=in_specs,
        out_specs=pl.BlockSpec((1, block, CAP, STEPS, 1, ZD, TY), lambda c, i: (0, i, 0, 0, first + c, 0, 0)),
        out_shape=jax.ShapeDtypeStruct((1, SPANS, CAP, STEPS, COMPS, ZD, TY), jnp.float32),
        input_output_aliases={} if so_far is None else {1: 0},
        compiler_params=pltpu.CompilerParams(vmem_limit_bytes=VMEM),
        name="inlet_tiles",
    )(received, *([] if so_far is None else [so_far]))


def after(values, others):
    return lax.optimization_barrier((*values, *others))[: len(values)] if others else values


def first_exchange(to_a, to_b):
    return lax.ppermute(to_a, "chan", PAIR_A), lax.ppermute(to_b, "chan", PAIR_B)


def for_second_exchange(kept, from_a, from_b):
    half = STEPS // 2
    for_b = (kept[:half] + from_a[half:].astype(jnp.float32)).astype(jnp.float16)
    for_a = (kept[half:] + from_b[half:].astype(jnp.float32)).astype(jnp.float16)
    return for_b, for_a


def second_exchange(for_b, for_a):
    return lax.ppermute(for_b, "chan", PAIR_B), lax.ppermute(for_a, "chan", PAIR_A)


def summed(own, from_a, from_b, second_b, second_a):
    half = STEPS // 2
    first = own[:half] + from_a[:half].astype(jnp.float32) + second_b.astype(jnp.float32)
    second = own[half:] + from_b[:half].astype(jnp.float32) + second_a.astype(jnp.float32)
    return first, second


def along_span(values):
    return lax.all_to_all(values, "span", split_axis=0, concat_axis=0, tiled=True)


def local(noise, widths, rms_profile, tile_owner):
    chan = lax.axis_index("chan").astype(jnp.int32).reshape(1)
    taps = vertical_filter_matrix(widths)
    taps_high = lax.reduce_precision(taps, 8, 7)
    taps_low = (taps - taps_high).astype(jnp.bfloat16)
    taps = (taps_high.astype(jnp.bfloat16), taps_low)
    rms = lax.dynamic_slice_in_dim(rms_profile, lax.axis_index("span") * ZD, ZD, 1)[:, :, None]
    owner = tile_owner[:, 0]
    tile = jnp.arange(SPANS, dtype=jnp.int32)
    earlier = (owner[:, None] == owner[None, :]) & (tile[None, :] < tile[:, None])
    slot = jnp.sum(earlier.astype(jnp.int32), axis=1)

    leave0 = time_filter(noise, chan, 0, True)
    leave1 = [v.astype(jnp.float16) for v in time_filter(noise, chan, 1, True)]
    stay0 = time_filter(noise, chan, 0, False)
    got0 = after(first_exchange(*leave0), (*leave1, *stay0, *taps, owner, slot, rms))
    got1 = first_exchange(*after(leave1, got0))
    sends0 = for_second_exchange(stay0[0], *got0)
    (chan,) = after((chan,), sends0)
    stay1 = time_filter(noise, chan, 1, False)
    leave2 = [v.astype(jnp.float16) for v in time_filter(noise, chan, 2, True)]
    got1 = after(got1, (*stay1, *leave2))
    sends1 = for_second_exchange(stay1[0], *got1)
    got2 = first_exchange(*after(leave2, sends1))
    (chan,) = after((chan,), sends1)
    stay2 = time_filter(noise, chan, 2, False)
    sends2 = for_second_exchange(stay2[0], *got2)
    sums = [
        summed(stay[1], *got, *second_exchange(*sends))
        for stay, got, sends in ((stay0, got0, sends0), (stay1, got1, sends1), (stay2, got2, sends2))
    ]
    sums[1] = after(sums[1], stay2)

    planes = None
    for c in range(2):
        planes = vertical_filter(taps, sums[c], (SPANS, ZD, 2 * WIDTH), (0, 0, c), planes)
    moved = along_span(planes)
    shape = (SPANS, 2 * CAP * ZD + ZD, WIDTH)
    mixed = vertical_filter(taps, sums[2], shape, (0, 2 * CAP, 0))
    mixed = along_span(span_filter(owner, slot, rms, moved, (0, 0), 0, 2, shape, mixed)[0])
    last, tiles = span_filter(
        owner, slot, rms, mixed, (2 * CAP, 0), 2, 1, (SPANS, CAP * ZD, WIDTH), keep=2 * CAP * ZD
    )
    return inlet_tiles(along_span(last), 2, 1, inlet_tiles(tiles, 0, 2))


def solution(mesh):
    in_specs = (P(None, "chan", "span", None), P(), P(), P("span", None))
    out_specs = P("span", None, None, "chan", None, None, None)
    return jax.shard_map(local, mesh=mesh, in_specs=in_specs, out_specs=out_specs, check_vma=False)
```

```python
import functools
import math

import jax
import jax.numpy as jnp
import ml_dtypes
import numpy as np
from jax import lax
from jax.experimental import pallas as pl
from jax.experimental.pallas import tpu as pltpu
from jax.sharding import PartitionSpec as P

Y = 2048
Z = 512
KT = 128
KY = 96
KZ = 48
NW = 4
TY = 64
COMPS = 3
STEPS = 8
PLANES = 40
CHANS = 4
SPANS = 32
CAP = 2
ZD = Z // SPANS
ROWS = 16
BLOCK = 32
LANES = 2 * TY
WIDTH = STEPS * TY
MIB = 1024 * 1024
TIME_VMEM = 57 * MIB
VMEM = 16 * MIB

PAIR_A = [(0, 1), (1, 0), (2, 3), (3, 2)]
PAIR_B = [(1, 2), (2, 1), (3, 0), (0, 3)]


def gaussian(offset, length_scale):
    return np.exp(-math.pi * offset * offset / (2.0 * length_scale * length_scale))


def time_taps():
    offset = np.arange(CHANS * PLANES)[None, :] - np.arange(CHANS * STEPS)[:, None]
    norm = np.sqrt(np.sum(gaussian(np.arange(KT) - KT // 2.0, KT / 4.0) ** 2))
    inside = (offset >= 0) & (offset < KT)
    return np.where(inside, gaussian(offset - KT // 2.0, KT / 4.0) / norm, 0.0)


def time_blocks():
    taps = time_taps().astype(np.float32).reshape(CHANS, STEPS, CHANS, PLANES)
    half = STEPS // 2
    blocks = []
    for d in range(CHANS):
        a, b, far = d ^ 1, CHANS - 1 - d, (d + 2) % CHANS
        first, second = slice(0, half), slice(half, STEPS)
        order = [(a, first), (far, first), (b, second), (far, second), (b, first), (a, second), (d, first), (d, second)]
        rows = np.concatenate([taps[block, steps, d] for block, steps in order])
        blocks.append(np.kron(rows, np.eye(ROWS, dtype=np.float32)))
    return np.stack(blocks).astype(ml_dtypes.bfloat16)


def split(values):
    high = values.astype(ml_dtypes.bfloat16)
    return high, (values - high.astype(np.float32)).astype(ml_dtypes.bfloat16)


def span_bands():
    taps = gaussian(np.arange(KY) - KY // 2.0, KY / 4.0)
    taps = taps / np.sqrt(np.sum(taps**2))
    bands = np.zeros((3, 2, TY, 2, TY), np.float32)
    for shift in range(3):
        tap = np.arange(TY)[:, None] + TY * (shift - 1) - np.arange(TY)[None, :] + KY // 2
        for step in range(2):
            bands[shift, step, :, step, :] = np.where((tap >= 0) & (tap < KY), taps[np.clip(tap, 0, KY - 1)], 0.0)
    return np.stack(split(bands.reshape(3, 2, TY, LANES)))


def vertical_filter_matrix(widths):
    def device_gaussian(offset, length_scale):
        offset_f = offset.astype(jnp.float32)
        return jnp.exp(-math.pi * offset_f * offset_f / (2.0 * length_scale * length_scale))

    offset = jnp.arange(Z)[None, :] - jnp.arange(Z)[:, None]
    length_scale = (KZ * (widths + 1)).astype(jnp.float32) / (4.0 * NW)
    tap_offsets = jnp.arange(KZ) - KZ // 2
    tap_norm = jnp.sqrt(
        jnp.sum(device_gaussian(tap_offsets[None, :], length_scale[:, None]) ** 2, axis=1)
    )
    inside = (offset >= -(KZ // 2)) & (offset < KZ - KZ // 2)
    return jnp.where(
        inside, device_gaussian(offset, length_scale[:, None]) / tap_norm[:, None], 0.0
    )


def time_kernel(chan_ref, taps_ref, noise_ref, *out_refs):
    for first in range(0, BLOCK, ROWS):
        rows = slice(first, first + ROWS)
        planes = noise_ref[:, :, rows].reshape(PLANES * ROWS, Z)
        sums = jnp.dot(taps_ref[0], planes, preferred_element_type=jnp.float32)
        sums = sums.reshape(2, STEPS, 1, ROWS, Z)
        for block, out_ref in enumerate(out_refs):
            out_ref[:, :, rows] = sums[block].astype(out_ref.dtype)


def time_filter(noise, chan, comp, leaving):
    out = pl.BlockSpec((STEPS, 1, BLOCK, Z), lambda j, chan: (0, 0, j, 0))
    part = 0 if leaving else 1
    kind = jnp.bfloat16 if leaving and comp == 0 else jnp.float32
    return pl.pallas_call(
        time_kernel,
        grid_spec=pltpu.PrefetchScalarGridSpec(
            num_scalar_prefetch=1,
            grid=(TY // BLOCK,),
            in_specs=[
                pl.BlockSpec((1, 2 * STEPS * ROWS, PLANES * ROWS), lambda j, chan: (chan[0], part, 0)),
                pl.BlockSpec((1, PLANES, BLOCK, Z), lambda j, chan: (comp, 0, j, 0)),
            ],
            out_specs=[out] * 2,
        ),
        out_shape=[jax.ShapeDtypeStruct((STEPS, 1, TY, Z), kind)] * 2,
        compiler_params=pltpu.CompilerParams(vmem_limit_bytes=TIME_VMEM),
        name="time_filter",
    )(chan, time_blocks(), noise)


def vertical_kernel(high_ref, low_ref, first_ref, second_ref, *refs):
    out_ref = refs[-1]
    timed = jnp.concatenate([first_ref[...], second_ref[...]]).reshape(STEPS * TY, Z)
    timed_high = timed.astype(jnp.bfloat16)
    timed_low = (timed - timed_high.astype(jnp.float32)).astype(jnp.bfloat16)

    def product(taps, values):
        return lax.dot_general(taps, values, (((1,), (1,)), ((), ())), preferred_element_type=jnp.float32)

    total = product(high_ref[...], timed_low) + product(low_ref[...], timed_high)
    total = total + product(high_ref[...], timed_high)
    out_ref[...] = total.astype(jnp.bfloat16).reshape(out_ref.shape)


def vertical_filter(taps, sums, shape, place, so_far=None):
    half = pl.BlockSpec((STEPS // 2, 1, TY, Z), lambda i: (0, 0, 0, 0))
    in_specs = [pl.BlockSpec((Z, Z), lambda i: (0, 0))] * 2 + [half] * 2
    if so_far is not None:
        in_specs.append(pl.BlockSpec(memory_space=pl.ANY))
    return pl.pallas_call(
        vertical_kernel,
        grid=(1,),
        in_specs=in_specs,
        out_specs=pl.BlockSpec((SPANS, ZD, WIDTH), lambda i: place),
        out_shape=jax.ShapeDtypeStruct(shape, jnp.bfloat16),
        input_output_aliases={} if so_far is None else {4: 0},
        compiler_params=pltpu.CompilerParams(vmem_limit_bytes=VMEM),
        name="vertical_filter",
    )(*taps, *sums, *([] if so_far is None else [so_far]))


def span_kernel(keep, owner_ref, slot_ref, bands_ref, rms_ref, x_ref, *refs):
    if keep:
        whole_ref, out_ref, kept_ref, taps_ref, sem = refs
        copy = pltpu.make_async_copy(whole_ref.at[:, : kept_ref.shape[1]], kept_ref, sem)
        copy.start()
    else:
        out_ref, taps_ref, sem = refs[-3:]

    @pl.when(pl.program_id(0) == 0)
    def _():
        for part in range(2):
            for source in range(4):
                for step in range(2):
                    rows = pl.ds((source % 2) * LANES + step * TY, TY)
                    for target in range(2):
                        shift = source - target
                        columns = pl.ds(target * LANES, LANES)
                        band = bands_ref[part, shift, step] if 0 <= shift < 3 else jnp.zeros((TY, LANES), jnp.bfloat16)
                        taps_ref[part, source // 2, rows, columns] = band

    out_ref[...] = jnp.zeros_like(out_ref)
    pairs = SPANS // 2
    for first in range(0, WIDTH, LANES):
        lanes = slice(first, first + LANES)
        x = x_ref[:, :, lanes]
        around = jnp.concatenate([x[SPANS - 1 :], x, x[:1]], axis=0).reshape(pairs + 1, 2, ZD, LANES)
        total = None
        for part in (1, 0):
            for half in range(2):
                tiles = [around[half : half + pairs, tile] for tile in range(2)]
                rows = jnp.concatenate(tiles, axis=-1).reshape(pairs * ZD, 2 * LANES)
                term = jnp.dot(rows, taps_ref[part, half], preferred_element_type=jnp.float32)
                total = term if total is None else total + term
        velocity = (total.reshape(pairs, ZD, 2 * LANES) * rms_ref[...]).astype(jnp.bfloat16)
        for i in range(SPANS):
            target = (i % 2) * LANES
            rows = pl.ds(pl.multiple_of(slot_ref[i] * ZD, ZD), ZD)
            out_ref[owner_ref[i], rows, lanes] = velocity[i // 2, :, target : target + LANES]
    if keep:
        copy.wait()


def span_filter(owner, slot, rms, moved, row, first, comps, shape, so_far=None, keep=0):
    in_specs = [
        pl.BlockSpec(memory_space=pltpu.SMEM),
        pl.BlockSpec(memory_space=pltpu.SMEM),
        pl.BlockSpec((2, 3, 2, TY, LANES), lambda i: (0, 0, 0, 0, 0)),
        pl.BlockSpec((1, ZD, 1), lambda i: (first + i, 0, 0)),
        pl.BlockSpec((SPANS, ZD, WIDTH), lambda i: (0, row + i, 0)),
    ]
    out_specs = [pl.BlockSpec((SPANS, CAP * ZD, WIDTH), lambda i: (0, i, 0))]
    out_shape = [jax.ShapeDtypeStruct(shape, jnp.bfloat16)]
    more = []
    if so_far is not None:
        in_specs.append(pl.BlockSpec(memory_space=pl.ANY))
        more.append(so_far)
    if keep:
        in_specs.append(pl.BlockSpec(memory_space=pl.ANY))
        more.append(moved)
        out_specs.append(pl.BlockSpec(memory_space=pl.ANY))
        out_shape.append(jax.ShapeDtypeStruct((SPANS, keep, WIDTH), jnp.bfloat16))
    return pl.pallas_call(
        functools.partial(span_kernel, keep > 0),
        grid=(comps,),
        in_specs=in_specs,
        out_specs=out_specs,
        out_shape=out_shape,
        input_output_aliases={} if so_far is None else {5: 0},
        scratch_shapes=[pltpu.VMEM((2, 2, 2 * LANES, 2 * LANES), jnp.bfloat16), pltpu.SemaphoreType.DMA],
        compiler_params=pltpu.CompilerParams(vmem_limit_bytes=VMEM),
        name="span_filter",
    )(owner, slot, span_bands(), rms, moved, *more)


def inlet_kernel(x_ref, *refs):
    out_ref = refs[-1]
    for slot in range(CAP):
        for s in range(STEPS):
            tile = x_ref[:, slot * ZD : (slot + 1) * ZD, s * TY : (s + 1) * TY]
            out_ref[0, :, slot, s, 0] = tile.astype(jnp.float32)


def inlet_tiles(received, first, comps, so_far=None):
    block = 8
    in_specs = [pl.BlockSpec((block, CAP * ZD, WIDTH), lambda c, i: (i, c, 0))]
    if so_far is not None:
        in_specs.append(pl.BlockSpec(memory_space=pl.ANY))
    return pl.pallas_call(
        inlet_kernel,
        grid=(comps, SPANS // block),
        in_specs=in_specs,
        out_specs=pl.BlockSpec((1, block, CAP, STEPS, 1, ZD, TY), lambda c, i: (0, i, 0, 0, first + c, 0, 0)),
        out_shape=jax.ShapeDtypeStruct((1, SPANS, CAP, STEPS, COMPS, ZD, TY), jnp.float32),
        input_output_aliases={} if so_far is None else {1: 0},
        compiler_params=pltpu.CompilerParams(vmem_limit_bytes=VMEM),
        name="inlet_tiles",
    )(received, *([] if so_far is None else [so_far]))


def after(values, others):
    return lax.optimization_barrier((*values, *others))[: len(values)] if others else values


def first_exchange(to_a, to_b):
    return lax.ppermute(to_a, "chan", PAIR_A), lax.ppermute(to_b, "chan", PAIR_B)


def for_second_exchange(kept, from_a, from_b):
    half = STEPS // 2
    for_b = (kept[:half] + from_a[half:].astype(jnp.float32)).astype(jnp.float16)
    for_a = (kept[half:] + from_b[half:].astype(jnp.float32)).astype(jnp.float16)
    return for_b, for_a


def second_exchange(for_b, for_a):
    return lax.ppermute(for_b, "chan", PAIR_B), lax.ppermute(for_a, "chan", PAIR_A)


def summed(own, from_a, from_b, second_b, second_a):
    half = STEPS // 2
    first = own[:half] + from_a[:half].astype(jnp.float32) + second_b.astype(jnp.float32)
    second = own[half:] + from_b[:half].astype(jnp.float32) + second_a.astype(jnp.float32)
    return first, second


def along_span(values):
    return lax.all_to_all(values, "span", split_axis=0, concat_axis=0, tiled=True)


def local(noise, widths, rms_profile, tile_owner):
    chan = lax.axis_index("chan").astype(jnp.int32).reshape(1)
    taps = vertical_filter_matrix(widths)
    taps_high = lax.reduce_precision(taps, 8, 7)
    taps_low = (taps - taps_high).astype(jnp.bfloat16)
    taps = (taps_high.astype(jnp.bfloat16), taps_low)
    rms = lax.dynamic_slice_in_dim(rms_profile, lax.axis_index("span") * ZD, ZD, 1)[:, :, None]
    owner = tile_owner[:, 0]
    tile = jnp.arange(SPANS, dtype=jnp.int32)
    earlier = (owner[:, None] == owner[None, :]) & (tile[None, :] < tile[:, None])
    slot = jnp.sum(earlier.astype(jnp.int32), axis=1)

    leave0 = time_filter(noise, chan, 0, True)
    leave1 = [v.astype(jnp.float16) for v in time_filter(noise, chan, 1, True)]
    stay0, stay1 = [time_filter(noise, chan, c, False) for c in range(2)]
    got0 = after(first_exchange(*leave0), (*leave1, *stay0, *stay1, *taps, owner, slot, rms))
    got1 = first_exchange(*after(leave1, got0))
    sends0 = for_second_exchange(stay0[0], *got0)
    (chan,) = after((chan,), sends0)
    leave2 = [v.astype(jnp.float16) for v in time_filter(noise, chan, 2, True)]
    stay2 = time_filter(noise, chan, 2, False)
    got1 = after(got1, (*leave2, *stay2))
    sends1 = for_second_exchange(stay1[0], *got1)
    got2 = first_exchange(*after(leave2, sends1))
    sends2 = for_second_exchange(stay2[0], *got2)
    sums = [
        summed(stay[1], *got, *second_exchange(*sends))
        for stay, got, sends in ((stay0, got0, sends0), (stay1, got1, sends1), (stay2, got2, sends2))
    ]

    planes = None
    for c in range(2):
        planes = vertical_filter(taps, sums[c], (SPANS, 2 * ZD, WIDTH), (0, c, 0), planes)
    moved = along_span(planes)
    shape = (SPANS, 2 * CAP * ZD + ZD, WIDTH)
    mixed = vertical_filter(taps, sums[2], shape, (0, 2 * CAP, 0))
    mixed = along_span(span_filter(owner, slot, rms, moved, 0, 0, 2, shape, mixed)[0])
    last, tiles = span_filter(
        owner, slot, rms, mixed, 2 * CAP, 2, 1, (SPANS, CAP * ZD, WIDTH), keep=2 * CAP * ZD
    )
    return inlet_tiles(along_span(last), 2, 1, inlet_tiles(tiles, 0, 2))


def solution(mesh):
    in_specs = (P(None, "chan", "span", None), P(), P(), P("span", None))
    out_specs = P("span", None, None, "chan", None, None, None)
    return jax.shard_map(local, mesh=mesh, in_specs=in_specs, out_specs=out_specs, check_vma=False)
```

```python
import functools
import math

import jax
import jax.numpy as jnp
import ml_dtypes
import numpy as np
from jax import lax
from jax.experimental import pallas as pl
from jax.experimental.pallas import tpu as pltpu
from jax.sharding import PartitionSpec as P

Y = 2048
Z = 512
KT = 128
KY = 96
KZ = 48
NW = 4
TY = 64
COMPS = 3
STEPS = 8
PLANES = 40
CHANS = 4
SPANS = 32
CAP = 2
ZD = Z // SPANS
ROWS = 16
BLOCK = 32
LANES = 2 * TY
WIDTH = STEPS * TY
MIB = 1024 * 1024
TIME_VMEM = 57 * MIB
VMEM = 16 * MIB

PAIR_A = [(0, 1), (1, 0), (2, 3), (3, 2)]
PAIR_B = [(1, 2), (2, 1), (3, 0), (0, 3)]


def gaussian(offset, length_scale):
    return np.exp(-math.pi * offset * offset / (2.0 * length_scale * length_scale))


def time_taps():
    offset = np.arange(CHANS * PLANES)[None, :] - np.arange(CHANS * STEPS)[:, None]
    norm = np.sqrt(np.sum(gaussian(np.arange(KT) - KT // 2.0, KT / 4.0) ** 2))
    inside = (offset >= 0) & (offset < KT)
    return np.where(inside, gaussian(offset - KT // 2.0, KT / 4.0) / norm, 0.0)


def time_blocks():
    taps = time_taps().astype(np.float32).reshape(CHANS, STEPS, CHANS, PLANES)
    half = STEPS // 2
    blocks = []
    for d in range(CHANS):
        a, b, far = d ^ 1, CHANS - 1 - d, (d + 2) % CHANS
        first, second = slice(0, half), slice(half, STEPS)
        order = [(a, first), (far, first), (b, second), (far, second), (b, first), (a, second), (d, first), (d, second)]
        rows = np.concatenate([taps[block, steps, d] for block, steps in order])
        blocks.append(np.kron(rows, np.eye(ROWS, dtype=np.float32)))
    return np.stack(blocks).astype(ml_dtypes.bfloat16)


def split(values):
    high = values.astype(ml_dtypes.bfloat16)
    return high, (values - high.astype(np.float32)).astype(ml_dtypes.bfloat16)


def span_bands():
    taps = gaussian(np.arange(KY) - KY // 2.0, KY / 4.0)
    taps = taps / np.sqrt(np.sum(taps**2))
    bands = np.zeros((3, 2, TY, 2, TY), np.float32)
    for shift in range(3):
        tap = np.arange(TY)[:, None] + TY * (shift - 1) - np.arange(TY)[None, :] + KY // 2
        for step in range(2):
            bands[shift, step, :, step, :] = np.where((tap >= 0) & (tap < KY), taps[np.clip(tap, 0, KY - 1)], 0.0)
    return np.stack(split(bands.reshape(3, 2, TY, LANES)))


def vertical_filter_matrix(widths):
    def device_gaussian(offset, length_scale):
        offset_f = offset.astype(jnp.float32)
        return jnp.exp(-math.pi * offset_f * offset_f / (2.0 * length_scale * length_scale))

    offset = jnp.arange(Z)[None, :] - jnp.arange(Z)[:, None]
    length_scale = (KZ * (widths + 1)).astype(jnp.float32) / (4.0 * NW)
    tap_offsets = jnp.arange(KZ) - KZ // 2
    tap_norm = jnp.sqrt(
        jnp.sum(device_gaussian(tap_offsets[None, :], length_scale[:, None]) ** 2, axis=1)
    )
    inside = (offset >= -(KZ // 2)) & (offset < KZ - KZ // 2)
    return jnp.where(
        inside, device_gaussian(offset, length_scale[:, None]) / tap_norm[:, None], 0.0
    )


def time_kernel(chan_ref, taps_ref, noise_ref, *out_refs):
    for first in range(0, BLOCK, ROWS):
        rows = slice(first, first + ROWS)
        planes = noise_ref[:, :, rows].reshape(PLANES * ROWS, Z)
        sums = jnp.dot(taps_ref[0], planes, preferred_element_type=jnp.float32)
        sums = sums.reshape(2, STEPS, 1, ROWS, Z)
        for block, out_ref in enumerate(out_refs):
            out_ref[:, :, rows] = sums[block].astype(out_ref.dtype)


def time_filter(noise, chan, comp, leaving):
    out = pl.BlockSpec((STEPS, 1, BLOCK, Z), lambda j, chan: (0, 0, j, 0))
    part = 0 if leaving else 1
    kind = jnp.bfloat16 if leaving and comp == 0 else jnp.float32
    return pl.pallas_call(
        time_kernel,
        grid_spec=pltpu.PrefetchScalarGridSpec(
            num_scalar_prefetch=1,
            grid=(TY // BLOCK,),
            in_specs=[
                pl.BlockSpec((1, 2 * STEPS * ROWS, PLANES * ROWS), lambda j, chan: (chan[0], part, 0)),
                pl.BlockSpec((1, PLANES, BLOCK, Z), lambda j, chan: (comp, 0, j, 0)),
            ],
            out_specs=[out] * 2,
        ),
        out_shape=[jax.ShapeDtypeStruct((STEPS, 1, TY, Z), kind)] * 2,
        compiler_params=pltpu.CompilerParams(vmem_limit_bytes=TIME_VMEM),
        name="time_filter",
    )(chan, time_blocks(), noise)


def vertical_kernel(high_ref, low_ref, first_ref, second_ref, *refs):
    out_ref = refs[-1]
    timed = jnp.concatenate([first_ref[...], second_ref[...]]).reshape(STEPS * TY, Z)
    timed_high = timed.astype(jnp.bfloat16)
    timed_low = (timed - timed_high.astype(jnp.float32)).astype(jnp.bfloat16)

    def product(taps, values):
        return lax.dot_general(taps, values, (((1,), (1,)), ((), ())), preferred_element_type=jnp.float32)

    total = product(high_ref[...], timed_low) + product(low_ref[...], timed_high)
    total = total + product(high_ref[...], timed_high)
    out_ref[...] = total.astype(jnp.bfloat16).reshape(out_ref.shape)


def vertical_filter(taps, sums, shape, place, so_far=None):
    half = pl.BlockSpec((STEPS // 2, 1, TY, Z), lambda i: (0, 0, 0, 0))
    in_specs = [pl.BlockSpec((Z, Z), lambda i: (0, 0))] * 2 + [half] * 2
    if so_far is not None:
        in_specs.append(pl.BlockSpec(memory_space=pl.ANY))
    return pl.pallas_call(
        vertical_kernel,
        grid=(1,),
        in_specs=in_specs,
        out_specs=pl.BlockSpec((SPANS, ZD, WIDTH), lambda i: place),
        out_shape=jax.ShapeDtypeStruct(shape, jnp.bfloat16),
        input_output_aliases={} if so_far is None else {4: 0},
        compiler_params=pltpu.CompilerParams(vmem_limit_bytes=VMEM),
        name="vertical_filter",
    )(*taps, *sums, *([] if so_far is None else [so_far]))


def span_kernel(keep, owner_ref, slot_ref, bands_ref, rms_ref, x_ref, *refs):
    if keep:
        whole_ref, out_ref, kept_ref, taps_ref, sem = refs
        copy = pltpu.make_async_copy(whole_ref.at[:, : kept_ref.shape[1]], kept_ref, sem)
        copy.start()
    else:
        out_ref, taps_ref, sem = refs[-3:]

    @pl.when(pl.program_id(0) == 0)
    def _():
        for part in range(2):
            for source in range(4):
                for step in range(2):
                    rows = pl.ds((source % 2) * LANES + step * TY, TY)
                    for target in range(2):
                        shift = source - target
                        columns = pl.ds(target * LANES, LANES)
                        band = bands_ref[part, shift, step] if 0 <= shift < 3 else jnp.zeros((TY, LANES), jnp.bfloat16)
                        taps_ref[part, source // 2, rows, columns] = band

    out_ref[...] = jnp.zeros_like(out_ref)
    pairs = SPANS // 2
    for first in range(0, WIDTH, LANES):
        lanes = slice(first, first + LANES)
        x = x_ref[:, :, lanes]
        around = jnp.concatenate([x[SPANS - 1 :], x, x[:1]], axis=0).reshape(pairs + 1, 2, ZD, LANES)
        total = None
        for part in (1, 0):
            for half in range(2):
                tiles = [around[half : half + pairs, tile] for tile in range(2)]
                rows = jnp.concatenate(tiles, axis=-1).reshape(pairs * ZD, 2 * LANES)
                term = jnp.dot(rows, taps_ref[part, half], preferred_element_type=jnp.float32)
                total = term if total is None else total + term
        velocity = (total.reshape(pairs, ZD, 2 * LANES) * rms_ref[...]).astype(jnp.bfloat16)
        for i in range(SPANS):
            target = (i % 2) * LANES
            rows = pl.ds(pl.multiple_of(slot_ref[i] * ZD, ZD), ZD)
            out_ref[owner_ref[i], rows, lanes] = velocity[i // 2, :, target : target + LANES]
    if keep:
        copy.wait()


def span_filter(owner, slot, rms, moved, row, first, comps, shape, so_far=None, keep=0):
    in_specs = [
        pl.BlockSpec(memory_space=pltpu.SMEM),
        pl.BlockSpec(memory_space=pltpu.SMEM),
        pl.BlockSpec((2, 3, 2, TY, LANES), lambda i: (0, 0, 0, 0, 0)),
        pl.BlockSpec((1, ZD, 1), lambda i: (first + i, 0, 0)),
        pl.BlockSpec((SPANS, ZD, WIDTH), lambda i: (0, row + i, 0)),
    ]
    out_specs = [pl.BlockSpec((SPANS, CAP * ZD, WIDTH), lambda i: (0, i, 0))]
    out_shape = [jax.ShapeDtypeStruct(shape, jnp.bfloat16)]
    more = []
    if so_far is not None:
        in_specs.append(pl.BlockSpec(memory_space=pl.ANY))
        more.append(so_far)
    if keep:
        in_specs.append(pl.BlockSpec(memory_space=pl.ANY))
        more.append(moved)
        out_specs.append(pl.BlockSpec(memory_space=pl.ANY))
        out_shape.append(jax.ShapeDtypeStruct((SPANS, keep, WIDTH), jnp.bfloat16))
    return pl.pallas_call(
        functools.partial(span_kernel, keep > 0),
        grid=(comps,),
        in_specs=in_specs,
        out_specs=out_specs,
        out_shape=out_shape,
        input_output_aliases={} if so_far is None else {5: 0},
        scratch_shapes=[pltpu.VMEM((2, 2, 2 * LANES, 2 * LANES), jnp.bfloat16), pltpu.SemaphoreType.DMA],
        compiler_params=pltpu.CompilerParams(vmem_limit_bytes=VMEM),
        name="span_filter",
    )(owner, slot, span_bands(), rms, moved, *more)


def inlet_kernel(x_ref, *refs):
    out_ref = refs[-1]
    for slot in range(CAP):
        for s in range(STEPS):
            tile = x_ref[:, slot * ZD : (slot + 1) * ZD, s * TY : (s + 1) * TY]
            out_ref[0, :, slot, s, 0] = tile.astype(jnp.float32)


def inlet_tiles(received, first, comps, so_far=None):
    block = 8
    in_specs = [pl.BlockSpec((block, CAP * ZD, WIDTH), lambda c, i: (i, c, 0))]
    if so_far is not None:
        in_specs.append(pl.BlockSpec(memory_space=pl.ANY))
    return pl.pallas_call(
        inlet_kernel,
        grid=(comps, SPANS // block),
        in_specs=in_specs,
        out_specs=pl.BlockSpec((1, block, CAP, STEPS, 1, ZD, TY), lambda c, i: (0, i, 0, 0, first + c, 0, 0)),
        out_shape=jax.ShapeDtypeStruct((1, SPANS, CAP, STEPS, COMPS, ZD, TY), jnp.float32),
        input_output_aliases={} if so_far is None else {1: 0},
        compiler_params=pltpu.CompilerParams(vmem_limit_bytes=VMEM),
        name="inlet_tiles",
    )(received, *([] if so_far is None else [so_far]))


def after(values, others):
    return lax.optimization_barrier((*values, *others))[: len(values)] if others else values


def first_exchange(to_a, to_b):
    return lax.ppermute(to_a, "chan", PAIR_A), lax.ppermute(to_b, "chan", PAIR_B)


def for_second_exchange(kept, from_a, from_b):
    half = STEPS // 2
    for_b = (kept[:half] + from_a[half:].astype(jnp.float32)).astype(jnp.float16)
    for_a = (kept[half:] + from_b[half:].astype(jnp.float32)).astype(jnp.float16)
    return for_b, for_a


def second_exchange(for_b, for_a):
    return lax.ppermute(for_b, "chan", PAIR_B), lax.ppermute(for_a, "chan", PAIR_A)


def summed(own, from_a, from_b, second_b, second_a):
    half = STEPS // 2
    first = own[:half] + from_a[:half].astype(jnp.float32) + second_b.astype(jnp.float32)
    second = own[half:] + from_b[:half].astype(jnp.float32) + second_a.astype(jnp.float32)
    return first, second


def along_span(values):
    return lax.all_to_all(values, "span", split_axis=0, concat_axis=0, tiled=True)


def local(noise, widths, rms_profile, tile_owner):
    chan = lax.axis_index("chan").astype(jnp.int32).reshape(1)
    taps = vertical_filter_matrix(widths)
    taps_high = lax.reduce_precision(taps, 8, 7)
    taps_low = (taps - taps_high).astype(jnp.bfloat16)
    taps = (taps_high.astype(jnp.bfloat16), taps_low)
    rms = lax.dynamic_slice_in_dim(rms_profile, lax.axis_index("span") * ZD, ZD, 1)[:, :, None]
    owner = tile_owner[:, 0]
    tile = jnp.arange(SPANS, dtype=jnp.int32)
    earlier = (owner[:, None] == owner[None, :]) & (tile[None, :] < tile[:, None])
    slot = jnp.sum(earlier.astype(jnp.int32), axis=1)

    leave0 = time_filter(noise, chan, 0, True)
    leave1 = [v.astype(jnp.float16) for v in time_filter(noise, chan, 1, True)]
    stay0, stay1 = [time_filter(noise, chan, c, False) for c in range(2)]
    got0 = after(first_exchange(*leave0), (*leave1, *stay0, *stay1, *taps, owner, slot, rms))
    got1 = first_exchange(*after(leave1, got0))
    sends0 = for_second_exchange(stay0[0], *got0)
    (chan,) = after((chan,), sends0)
    leave2 = time_filter(noise, chan, 2, True)
    stay2 = time_filter(noise, chan, 2, False)
    got1 = after(got1, (*leave2, *stay2))
    sends1 = for_second_exchange(stay1[0], *got1)
    got2 = first_exchange(*[v.astype(jnp.float16) for v in after(leave2, sends1)])
    sends2 = for_second_exchange(stay2[0], *got2)
    sums = [
        summed(stay[1], *got, *second_exchange(*sends))
        for stay, got, sends in ((stay0, got0, sends0), (stay1, got1, sends1), (stay2, got2, sends2))
    ]

    planes = None
    for c in range(2):
        planes = vertical_filter(taps, sums[c], (SPANS, 2 * ZD, WIDTH), (0, c, 0), planes)
    moved = along_span(planes)
    shape = (SPANS, 2 * CAP * ZD + ZD, WIDTH)
    mixed = vertical_filter(taps, sums[2], shape, (0, 2 * CAP, 0))
    mixed = along_span(span_filter(owner, slot, rms, moved, 0, 0, 2, shape, mixed)[0])
    last, tiles = span_filter(
        owner, slot, rms, mixed, 2 * CAP, 2, 1, (SPANS, CAP * ZD, WIDTH), keep=2 * CAP * ZD
    )
    return inlet_tiles(along_span(last), 2, 1, inlet_tiles(tiles, 0, 2))


def solution(mesh):
    in_specs = (P(None, "chan", "span", None), P(), P(), P("span", None))
    out_specs = P("span", None, None, "chan", None, None, None)
    return jax.shard_map(local, mesh=mesh, in_specs=in_specs, out_specs=out_specs, check_vma=False)
```
